128 devices in a mesh: gz: 4 (over z), xy: 32 (over x, y, core).
Axes of the slice: x: 4, y: 4, z: 4, core: 2. Of those that a mesh axis runs over, the one named last changes fastest.
Arguments:
- volume: bfloat16 [512, 4096, 128], P('gz', 'xy'), may hold values from -6 to 6
- corners: int32 [3, 8192], P(None, ('gz', 'xy')), may hold values from 0 to 95
- destination: int32 [8192, 1], P(('gz', 'xy')), may hold values from 0 to 31; in each aligned block of 64 rows (0 to 63, 64 to 127, ...) at most 4 rows name the same one
- svx_ids: int32 [8192], P(('gz', 'xy')), may hold values from 0 to 4095
- svx_rows: int32 [4096], replicated, may hold values from 0 to 4095, each once
- stem_w: bfloat16 [3, 3, 3, 1, 64], replicated, may hold values from -1.25 to 1.25
- stem_b: float32 [64], replicated, may hold values from -3 to 3
- conv_w1: bfloat16 [3, 3, 3, 64, 64], replicated, may hold values from -0.15625 to 0.15625
- conv_b1: float32 [64], replicated, may hold values from -3 to 3
- conv_w2: bfloat16 [3, 3, 3, 64, 64], replicated, may hold values from -0.15625 to 0.15625
- conv_b2: float32 [64], replicated, may hold values from -3 to 3
- head_w: bfloat16 [64, 64], replicated, may hold values from -0.75 to 0.75
- head_b: float32 [64], replicated, may hold values from -3 to 3
Outputs:
- svx_sums: float32 [4096, 64], P('xy')
- worker_batch: float32 [16384, 64], P(('gz', 'xy'))
The draws below stay inside these ranges and needn't reach their ends.
Inputs may be any that keep to these rules, and one draw needn't show every extreme that they name: `destination`: no more than 4 sites of one device name one worker, and exactly 4 do for some worker of some devices. `svx_rows`: each row once.
All inputs are finite; a program needn't handle non-finite values.
Results may differ from the reference program's by a relative error of at most 0.0003.
Values may be sent and summed in bfloat16 or wider, within the bound.
No kernel may reach another device: no remote copies, remote signals or barrier semaphores. Data moves between devices by JAX's collectives and lax.ppermute only.
A program may use at most 320 MiB of HBM per device.

```python
import math
import jax
import jax.numpy as jnp
import numpy as np
from jax import lax

BLOCK = 128
CUT = 33
CH = 64
EMB = 64
SITES_DEV = 64
CAP = 4
SITES = 8192
SUPER = 4096
N_GZ = 4
N_XY = 32


def plant(drawn, own_key, least, high):
    longest = drawn.shape.index(max(drawn.shape))
    spots = []
    for shift in (0, 1):
        where = [jax.random.randint(jax.random.fold_in(own_key, axis), (), 0, length) for axis, length in enumerate(drawn.shape)]
        where[longest] = (where[longest] + shift) % drawn.shape[longest]
        spots.append(tuple(where))
    return drawn.at[spots[0]].set(least).at[spots[1]].set(high)


def shard_levels(stream_key, extent, pieces, smallest, high):
    level = 1.0
    for position, parts in pieces:
        heights = jax.random.uniform(jax.random.fold_in(jax.random.fold_in(stream_key, 6), position), (parts,), jnp.float32, smallest / len(pieces), high / len(pieces))
        level = level * jnp.repeat(jnp.exp(heights), extent[position] // parts).reshape((-1,) + (1,) * (len(extent) - 1 - position))
    return level


def deal_out(key, own, number, rows, number_of, top, reach, skew):
    sequence = jax.random.permutation(key, number_of)
    crowded, usual = portions_of(number_of, rows * top, reach, skew, True), portions_of(number_of, rows * top, reach, skew, False)
    places = jnp.arange(number_of)

    def named(lengths, turn):
        used = int((lengths > 0).sum())
        fixed = max(1, used // 4)
        shifted = fixed + (places - fixed + turn * (used - fixed)) % max(1, number_of - fixed)
        return jnp.zeros((number_of,), jnp.int32).at[sequence[jnp.where(places < fixed, places, shifted)]].set(jnp.asarray(lengths, jnp.int32))

    lengths = jnp.where(number % 4 == 0, named(crowded, number // 4), named(usual, number - number // 4 - 1))
    mixed = jax.random.permutation(jax.random.fold_in(own, 3), number_of)
    donor, taker = mixed[0:number_of // 2 * 2:2], mixed[1:number_of // 2 * 2:2]
    slack = jnp.minimum(lengths[donor] - 1, reach - lengths[taker]) // 2
    slack = jnp.where((donor == sequence[0]) | (taker == sequence[0]) | (lengths[taker] == 0), 0, jnp.maximum(slack, 0))
    shifted = jax.random.randint(jax.random.fold_in(own, 4), (number_of // 2,), 0, 1 << 20) % (slack + 1)
    lengths = lengths.at[donor].add(-shifted).at[taker].add(shifted)
    items = jnp.searchsorted(jnp.cumsum(lengths), jnp.arange(rows * top), side="right").astype(jnp.int32)
    listing = items.reshape(top, rows).T
    listing = listing[jax.random.permutation(jax.random.fold_in(own, 1), rows)]
    turn = jax.random.randint(jax.random.fold_in(own, 2), (rows, 1), 0, top)
    return jnp.take_along_axis(listing, (jnp.arange(top)[None, :] + turn) % top, axis=1)


def portions_of(amount, total, most, lean, full):
    loads = [(1 << 20) // math.isqrt(rank ** lean) + 1 for rank in range(1, amount + 1)]
    largest = most if full else min(most, max(-(-total // amount), total * loads[0] // sum(loads)))
    least = 1 if total - largest >= amount - 1 else 0
    holding, surplus = [largest] + [least] * (amount - 1), total - largest - least * (amount - 1)
    while surplus > 0:
        candidates = [i for i in range(1, amount) if holding[i] < largest] or [i for i in range(1, amount) if holding[i] < most]
        mass, left = sum([loads[i] for i in candidates]), surplus
        for i in candidates:
            addition = min(most - holding[i], max(1, left * loads[i] // mass), surplus)
            holding[i] = holding[i] + addition
            surplus = surplus - addition
    return np.array(holding)


def noise(rng, extent, width, limit, cuts=(), held_as=jnp.bfloat16):
    values = jax.random.normal(rng, extent, jnp.float32) * width
    if len(cuts) > 0:
        values = shard_levels(rng, extent, cuts, -0.22, 0.18) * values
    return jnp.clip(values, min=-limit, max=limit).astype(held_as)


def setup_inputs(seed: int = 0) -> dict:
    key_of = jax.random.split(jax.random.key(seed), 14)
    volume = noise(key_of[0], (BLOCK * N_GZ, BLOCK * N_XY, BLOCK), 1.0, 6.0, ((0, 4), (1, 32)))
    corners = plant(jax.random.randint(key_of[1], (3, SITES), 0, BLOCK - CUT + 1), jax.random.fold_in(key_of[1], 1), 0, BLOCK - CUT).astype(jnp.int32)
    destination_keys = jax.random.split(jax.random.fold_in(key_of[2], 1), SITES // SITES_DEV)
    destination_turns = jax.random.permutation(jax.random.fold_in(key_of[2], 3), SITES // SITES_DEV)
    destination = jax.vmap(lambda own, number: deal_out(jax.random.fold_in(key_of[2], 2), own, number, SITES_DEV, N_XY, 1, CAP, 2))(destination_keys, destination_turns).reshape((SITES, 1))
    svx_ids = plant(jax.random.randint(key_of[3], (SITES,), 0, SUPER), jax.random.fold_in(key_of[3], 1), 0, SUPER - 1).astype(jnp.int32)
    svx_rows = jax.random.permutation(key_of[4], SUPER).astype(jnp.int32)
    stem_w = noise(key_of[5], (3, 3, 3, 1, CH), 27 ** -0.5, 1.25)
    stem_b = noise(key_of[6], (CH,), 0.5, 3.0, (), jnp.float32)
    conv_w1 = noise(key_of[7], (3, 3, 3, CH, CH), (27 * CH) ** -0.5, 0.15625)
    conv_b1 = noise(key_of[8], (CH,), 0.5, 3.0, (), jnp.float32)
    conv_w2 = noise(key_of[9], (3, 3, 3, CH, CH), (27 * CH) ** -0.5, 0.15625)
    conv_b2 = noise(key_of[10], (CH,), 0.5, 3.0, (), jnp.float32)
    head_w = noise(key_of[11], (CH, EMB), CH ** -0.5, 0.75)
    head_b = noise(key_of[12], (EMB,), 0.5, 3.0, (), jnp.float32)
    return dict(volume=volume, corners=corners, destination=destination, svx_ids=svx_ids, svx_rows=svx_rows, stem_w=stem_w, stem_b=stem_b, conv_w1=conv_w1, conv_b1=conv_b1, conv_w2=conv_w2, conv_b2=conv_b2, head_w=head_w, head_b=head_b)


def convolve(field, kernel, stride, padding):
    return lax.conv_general_dilated(field.astype(jnp.float32), kernel.astype(jnp.float32), (stride, stride, stride), padding, dimension_numbers=("NDHWC", "DHWIO", "NDHWC"), precision=lax.Precision.HIGHEST)


def embed(cutouts, stem_w, stem_b, conv_w1, conv_b1, conv_w2, conv_b2, head_w, head_b):
    stem = jax.nn.relu(convolve(cutouts[..., None], stem_w, 2, "VALID") + stem_b).astype(jnp.bfloat16)
    pooled = lax.reduce_window(stem, jnp.array(-jnp.inf, jnp.bfloat16), lax.max, (1, 2, 2, 2, 1), (1, 2, 2, 2, 1), "VALID")
    inner = jax.nn.relu(convolve(pooled, conv_w1, 1, "SAME") + conv_b1).astype(jnp.bfloat16)
    block = jax.nn.relu(convolve(inner, conv_w2, 1, "SAME") + conv_b2 + pooled.astype(jnp.float32))
    mean_act = jnp.mean(block, axis=(1, 2, 3))
    return jnp.dot(mean_act, head_w.astype(jnp.float32), precision=lax.Precision.HIGHEST) + head_b


def reference(volume, corners, destination, svx_ids, svx_rows, stem_w, stem_b, conv_w1, conv_b1, conv_w2, conv_b2, head_w, head_b):
    devices = N_GZ * N_XY
    starts = corners.reshape(3, devices, SITES_DEV)
    device_ids = jnp.arange(devices, dtype=jnp.int32)
    base_z = (device_ids // N_XY) * BLOCK
    base_x = (device_ids % N_XY) * BLOCK

    def one_device(items):
        zc, xc, yc, bz, bx = items
        cutouts = jax.vmap(lambda a, b, c: lax.dynamic_slice(volume, (bz + a, bx + b, c), (CUT, CUT, CUT)))(zc, xc, yc)
        return embed(cutouts, stem_w, stem_b, conv_w1, conv_b1, conv_w2, conv_b2, head_w, head_b)

    embeddings = lax.map(one_device, (starts[0], starts[1], starts[2], base_z, base_x))
    dest = destination.reshape(devices, SITES_DEV)
    onehot = (dest[:, :, None] == jnp.arange(N_XY, dtype=jnp.int32)[None, None, :]).astype(jnp.int32)
    rank = jnp.sum((jnp.cumsum(onehot, axis=1) - onehot) * onehot, axis=2)
    slab = (device_ids // N_XY)[:, None]
    source = (device_ids % N_XY)[:, None]
    row = ((slab * N_XY + dest) * N_XY + source) * CAP + rank
    flat = embeddings.reshape(devices * SITES_DEV, EMB)
    worker_batch = jnp.zeros((devices * N_XY * CAP, EMB), jnp.float32).at[row.reshape(-1)].set(flat)
    targets = svx_rows[svx_ids]
    svx_sums = jnp.zeros((SUPER, EMB), jnp.float32).at[targets].add(flat)
    return svx_sums, worker_batch
```

```python
import functools
import jax
import jax.numpy as jnp
from jax import lax
from jax.experimental import pallas as pl
from jax.experimental.pallas import tpu as pltpu
from jax.sharding import PartitionSpec as P

F32, BF16 = jnp.float32, jnp.bfloat16
STEP = 17


def lanes_of(shape):
    return lax.broadcasted_iota(jnp.int32, shape, len(shape) - 1)


def toeplitz(w_ref, big_ref):
    zero = jnp.zeros((64, 64), BF16)
    for dz in range(3):
        for xi in range(4):
            for xo in range(2):
                dx = xi - xo
                if 0 <= dx <= 2:
                    w = [w_ref[(dz * 3 + dx) * 3 + dy] for dy in range(3)]
                    rows = [(w[1], w[0]), (w[2], w[1]), (w[0], zero), (zero, w[2])]
                    tile = jnp.concatenate([jnp.concatenate(r, axis=1) for r in rows], axis=0)
                else:
                    tile = jnp.zeros((256, 128), BF16)
                big_ref[dz * 4 + xi, :, xo * 128 : (xo + 1) * 128] = tile


def stem_weights(sw_ref, ws_ref):
    t = lax.broadcasted_iota(jnp.int32, (256, 32), 1)
    k = lax.broadcasted_iota(jnp.int32, (256, 32), 0)
    kz, kx, ky = t // 9, (t // 3) % 3, t % 3
    base = jnp.where(kz == 2, 128 + STEP * kx, STEP * (kz * 3 + kx)) + ky
    base = jnp.where(t < 27, base, -1000)
    taps = sw_ref[...]
    for pair in range(4):
        for par in range(2):
            cols = []
            for inner in range(2):
                sy = 4 * pair + 2 * inner + par
                hot = (k == base + 2 * sy).astype(F32).astype(BF16)
                cols.append(jnp.dot(hot, taps, preferred_element_type=F32).astype(BF16))
            at = (pair * 2 + par) * 128
            ws_ref[:, at : at + 128] = jnp.concatenate(cols, axis=1)


def kernel(sites, corners, vol, sw, sb, w1, b1, w2, b2, hw, hb, out, vf, ub, pf, pq1, pq2, ws, big1, big2, acc):
    def widen(z, c):
        vf[z] = vol[z].astype(F32)
        return c

    lax.fori_loop(0, 128, widen, 0)
    toeplitz(w1, big1)
    toeplitz(w2, big2)
    stem_weights(sw, ws)

    lane = lanes_of((16, 128))
    masks = [[lane < STEP * (j + 1) + 16 * h for j in range(5)] for h in range(2)]

    def build(site, slot):
        z0, x0, y0 = corners[0, site], corners[1, site], corners[2, site]
        shift = [lax.rem(STEP * j + 128 - y0, 128) for j in range(6)]
        for u in range(17):
            pieces = []
            for zp in range(2 if u < 16 else 1):
                for kx in range(3):
                    a = vf[z0 + 2 * u + zp, pl.ds(x0 + kx, 8, 4), :]
                    b = vf[z0 + 2 * u + zp, pl.ds(x0 + kx + 2, 8, 4), :]
                    p = jnp.concatenate([a, b], axis=0)
                    pieces.append(pltpu.roll(p, shift[zp * 3 + kx], 1))
            for h in range(2):
                v = pieces[-1]
                for j in reversed(range(len(pieces) - 1)):
                    v = jnp.where(masks[h][j], pieces[j], v)
                ub[slot, h, u] = v.astype(BF16)

    bias = jnp.concatenate([sb[...], sb[...]], axis=1)

    def stem(site, slot):
        for h in range(2):
            lhs = jnp.concatenate(
                [ub[slot, h, 0:16].reshape(256, 128), ub[slot, h, 1:17].reshape(256, 128)], axis=1
            )
            r = jnp.dot(lhs, ws[:, h * 512 : h * 512 + 512], preferred_element_type=F32)
            r = r.reshape(8, 4, 8, 512)
            m = jnp.maximum(jnp.maximum(r[:, 0], r[:, 1]), jnp.maximum(r[:, 2], r[:, 3]))
            for pair in range(2):
                v = jnp.maximum(m[:, :, pair * 256 : pair * 256 + 128], m[:, :, pair * 256 + 128 : pair * 256 + 256])
                v = jnp.maximum(v + bias[None], 0.0)
                for z in range(8):
                    pf[z, h * 2 + pair, pl.ds(site, 8, sites), :] = v[z]

    build(0, 0)

    def both(i, c):
        s = 2 * i
        build(s + 1, 1)
        stem(s, 0)
        build(jnp.minimum(s + 2, sites - 1), 0)
        stem(s + 1, 1)
        return c

    lax.fori_loop(0, sites // 2, both, 0)

    low = lanes_of((sites, 128)) < 64

    def halo(r):
        out = []
        zero = jnp.zeros((sites, 128), F32)
        for p in range(4):
            left = r[p - 1] if p > 0 else zero
            right = r[p + 1] if p < 3 else zero
            out.append(jnp.where(low, left, right))
        return out

    def pack(z, c):
        for x in range(8):
            v = [pf[z, p, x * sites : (x + 1) * sites, :] for p in range(4)]
            q = halo([pltpu.roll(t, 64, 1) for t in v])
            for p in range(4):
                pq1[z, x, p, :, 0:128] = v[p].astype(BF16)
                pq1[z, x, p, :, 128:256] = q[p].astype(BF16)
        return c

    lax.fori_loop(0, 8, pack, 0)

    def conv(src, big, z, dzs, xb):
        xis = [xi for xi in range(4) if 0 <= 2 * xb - 1 + xi < 8]
        total = None
        for dz in dzs:
            for xi in xis:
                lhs = src[z + dz - 1, 2 * xb - 1 + xi].reshape(4 * sites, 256)
                part = jnp.dot(lhs, big[dz * 4 + xi], preferred_element_type=F32)
                total = part if total is None else total + part
        return total

    bias1 = jnp.concatenate([b1[...]] * 4, axis=1)
    bias2 = jnp.concatenate([b2[...]] * 4, axis=1)

    def first(z, dzs):
        for xb in range(4):
            v = jnp.maximum(conv(pq1, big1, z, dzs, xb) + bias1, 0.0).reshape(4, sites, 256)
            for xo in range(2):
                t = [v[p, :, xo * 128 : xo * 128 + 128] for p in range(4)]
                q = halo([pltpu.roll(s, 64, 1) for s in t])
                for p in range(4):
                    pq2[z, 2 * xb + xo, p, :, 0:128] = t[p].astype(BF16)
                    pq2[z, 2 * xb + xo, p, :, 128:256] = q[p].astype(BF16)

    def second(z, dzs):
        for xb in range(4):
            v = conv(pq2, big2, z, dzs, xb) + bias2
            skip = jnp.concatenate([pq1[z, 2 * xb + xo, :, :, 0:128].reshape(4 * sites, 128) for xo in range(2)], axis=1)
            v = jnp.maximum(v + skip.astype(F32), 0.0).reshape(4, sites, 256)
            acc[...] += jnp.sum(v, axis=0)

    def over_z(step):
        step(0, (1, 2))
        lax.fori_loop(1, 7, lambda z, c: (step(z, (0, 1, 2)), c)[1], 0)
        step(7, (0, 1))

    over_z(first)
    acc[...] = jnp.zeros_like(acc)
    over_z(second)
    a = acc[...]
    mean = (a[:, 0:64] + a[:, 64:128] + a[:, 128:192] + a[:, 192:256]) * (1.0 / 512.0)
    own = jnp.dot(mean, hw[...].astype(F32), precision=lax.Precision.HIGHEST, preferred_element_type=F32) + hb[...]
    out[...] = jnp.concatenate([own[0 : sites // 2], own[sites // 2 :]], axis=1)


def embed(volume, corners, stem_w, stem_b, conv_w1, conv_b1, conv_w2, conv_b2, head_w, head_b):
    sites = corners.shape[1]
    sw = jnp.pad(stem_w.reshape(27, 64), ((0, 5), (0, 0)))
    vmem = pl.BlockSpec(memory_space=pltpu.VMEM)
    smem = pl.BlockSpec(memory_space=pltpu.SMEM)
    return pl.pallas_call(
        functools.partial(kernel, sites),
        out_shape=jax.ShapeDtypeStruct((sites // 2, 128), F32),
        in_specs=[smem] + [vmem] * 9,
        out_specs=vmem,
        scratch_shapes=[
            pltpu.VMEM((128, 128, 128), F32),
            pltpu.VMEM((2, 2, 17, 16, 128), BF16),
            pltpu.VMEM((8, 4, 8 * sites, 128), F32),
            pltpu.VMEM((8, 8, 4, sites, 256), BF16),
            pltpu.VMEM((8, 8, 4, sites, 256), BF16),
            pltpu.VMEM((256, 1024), BF16),
            pltpu.VMEM((12, 256, 256), BF16),
            pltpu.VMEM((12, 256, 256), BF16),
            pltpu.VMEM((sites, 256), F32),
        ],
        compiler_params=pltpu.CompilerParams(vmem_limit_bytes=56 * 1024 * 1024),
        cost_estimate=pl.CostEstimate(flops=30_000_000_000, bytes_accessed=6_000_000, transcendentals=0),
    )(
        corners, volume, sw, stem_b.reshape(1, 64), conv_w1.reshape(27, 64, 64), conv_b1.reshape(1, 64),
        conv_w2.reshape(27, 64, 64), conv_b2.reshape(1, 64), head_w, head_b.reshape(1, 64),
    )


def collect_kernel(n_xy, own_rows, me_ref, codes, table, *refs):
    pieces, (batch, sums, slot, hots) = refs[:-4], refs[-4:]
    me = me_ref[0]
    wide = 2 * n_xy
    dest = codes[...]
    valid = (dest == me).astype(F32)
    earlier = (lax.broadcasted_iota(jnp.int32, (64, 64), 0) < lax.broadcasted_iota(jnp.int32, (64, 64), 1)).astype(F32)
    rank = jnp.dot(valid, earlier, preferred_element_type=F32).astype(jnp.int32)
    source = lax.broadcasted_iota(jnp.int32, (wide, 64), 0) // 2
    row = jnp.where(dest == me, source * 4 + rank, -1)
    odd = lax.broadcasted_iota(jnp.int32, (wide, 64), 0) % 2 == 1
    slot[...] = jnp.where(odd, dest, row)
    t = table[...]
    want = lax.broadcasted_iota(jnp.int32, (own_rows, 128), 0) + me * own_rows
    found = jnp.zeros((own_rows, 128), jnp.int32)
    lane = lax.broadcasted_iota(jnp.int32, (own_rows, 128), 1)
    for r in range(t.shape[0]):
        found = found + jnp.where(t[r : r + 1, :] == want, lane + r * 128, 0)
    owned = jnp.sum(found, axis=1, keepdims=True)
    rows = lax.broadcasted_iota(jnp.int32, (own_rows, 128), 0)
    for g in range(n_xy // 4):
        for half in range(2):
            lows = [[], []]
            for q in range(4 * g, 4 * g + 4):
                at = slot[pl.ds(2 * jnp.bitwise_xor(me, q), 1), :]
                aid = slot[pl.ds(2 * jnp.bitwise_xor(me, q) + 1, 1), :]
                lows[0].append(at[:, half * 32 : half * 32 + 32])
                lows[1].append(aid[:, half * 32 : half * 32 + 32])
            w, s = [jnp.concatenate(x, axis=1) for x in lows]
            top = half * 2 * own_rows
            hots[top : top + own_rows, g * 128 : g * 128 + 128] = (rows == w).astype(F32).astype(BF16)
            hots[top + own_rows : top + 2 * own_rows, g * 128 : g * 128 + 128] = (
                (owned == s).astype(F32).astype(BF16)
            )
    total = jnp.zeros((4 * own_rows, 128), F32)
    at = 0
    for p in pieces:
        x = p[...]
        hi = x.astype(BF16)
        rest = x - hi.astype(F32)
        mid = rest.astype(BF16)
        low = (rest - mid.astype(F32)).astype(BF16)
        parts = jnp.dot(
            hots[:, at : at + x.shape[0]], jnp.concatenate([hi, mid, low], axis=1), preferred_element_type=F32
        )
        total = total + (parts[:, 0:128] + (parts[:, 128:256] + parts[:, 256:384]))
        at += x.shape[0]
    n = own_rows
    batch[...] = total[0:n, 0:64] + total[2 * n : 3 * n, 64:128]
    mine = total[n : 2 * n, 0:64] + total[3 * n : 4 * n, 64:128]
    sums[...] = jnp.concatenate([mine[0 : n // 2], mine[n // 2 :]], axis=1)


def collect(pieces, codes, table, me, n_xy):
    own_rows = table.size // n_xy
    vmem = pl.BlockSpec(memory_space=pltpu.VMEM)
    return pl.pallas_call(
        functools.partial(collect_kernel, n_xy, own_rows),
        out_shape=(
            jax.ShapeDtypeStruct((own_rows, 64), F32),
            jax.ShapeDtypeStruct((own_rows // 2, 128), F32),
        ),
        in_specs=[pl.BlockSpec(memory_space=pltpu.SMEM)] + [vmem] * (2 + len(pieces)),
        out_specs=(vmem, vmem),
        scratch_shapes=[
            pltpu.VMEM((2 * n_xy, 64), jnp.int32),
            pltpu.VMEM((4 * own_rows, n_xy * 32), BF16),
        ],
        compiler_params=pltpu.CompilerParams(vmem_limit_bytes=32 * 1024 * 1024),
    )(me, codes, table, *pieces)


def body(
    volume, corners, destination, svx_ids, svx_rows,
    stem_w, stem_b, conv_w1, conv_b1, conv_w2, conv_b2, head_w, head_b,
):
    n_xy, n_gz = lax.axis_size("xy"), lax.axis_size("gz")

    def swap(a, k, axis="xy", n=n_xy):
        return lax.ppermute(a, axis, [(i, i ^ k) for i in range(n)])

    codes = lax.all_gather(jnp.stack([destination[:, 0], svx_ids]), "xy", tiled=True)
    own = embed(volume, corners, stem_w, stem_b, conv_w1, conv_b1, conv_w2, conv_b2, head_w, head_b)
    a = jnp.concatenate([own, swap(own, 1)])
    a = jnp.concatenate([a, swap(a, 2), swap(a, 4), swap(a, 6)])
    pieces = [a, swap(a, 8), swap(a, 16), swap(a, 24)]
    me = lax.axis_index("xy").astype(jnp.int32).reshape(1)
    batch, part = collect(pieces, codes, svx_rows.reshape(-1, 128), me, n_xy)
    z = [part] + [swap(part, k, "gz", n_gz) for k in (1, 2, 3)]
    total = (z[0] + z[1]) + (z[2] + z[3])
    return jnp.concatenate([total[:, 0:64], total[:, 64:128]]), batch


def solution(mesh):
    sites = P(("gz", "xy"))
    placed = (P("gz", "xy", None), P(None, ("gz", "xy")), P(("gz", "xy"), None), sites) + (P(),) * 9
    return jax.shard_map(
        body, mesh=mesh, in_specs=placed, out_specs=(P("xy", None), P(("gz", "xy"), None)), check_vma=False
    )
```

```python
import functools
import jax
import jax.numpy as jnp
from jax import lax
from jax.experimental import pallas as pl
from jax.experimental.pallas import tpu as pltpu
from jax.sharding import PartitionSpec as P

F32, BF16 = jnp.float32, jnp.bfloat16
STEP = 17
GROUP = 16


def lanes_of(shape):
    return lax.broadcasted_iota(jnp.int32, shape, len(shape) - 1)


def toeplitz(w_ref, big_ref):
    zero = jnp.zeros((64, 64), BF16)
    for dz in range(3):
        for xi in range(4):
            for xo in range(2):
                dx = xi - xo
                if 0 <= dx <= 2:
                    w = [w_ref[(dz * 3 + dx) * 3 + dy] for dy in range(3)]
                    rows = [(w[1], w[0]), (w[2], w[1]), (w[0], zero), (zero, w[2])]
                    tile = jnp.concatenate([jnp.concatenate(r, axis=1) for r in rows], axis=0)
                else:
                    tile = jnp.zeros((256, 128), BF16)
                big_ref[dz * 4 + xi, :, xo * 128 : (xo + 1) * 128] = tile


def stem_weights(taps, ws_ref):
    t = lax.broadcasted_iota(jnp.int32, (256, 32), 1)
    k = lax.broadcasted_iota(jnp.int32, (256, 32), 0)
    kz, kx, ky = t // 9, (t // 3) % 3, t % 3
    base = jnp.where(kz == 2, 128 + STEP * kx, STEP * (kz * 3 + kx)) + ky
    base = jnp.where(t < 27, base, -1000)
    for pair in range(4):
        for par in range(2):
            cols = []
            for inner in range(2):
                sy = 4 * pair + 2 * inner + par
                hot = (k == base + 2 * sy).astype(F32).astype(BF16)
                cols.append(jnp.dot(hot, taps, preferred_element_type=F32).astype(BF16))
            at = (pair * 2 + par) * 128
            ws_ref[:, at : at + 128] = jnp.concatenate(cols, axis=1)


def kernel(sites, corners, vol, sw, sb, w1, b1, w2, b2, hw, hb, dest, ids, out, vf, ub, taps, pf0, pf1, pq1, pq2, ws, big1, big2, acc):
    def widen(z, c):
        vf[z] = vol[z].astype(F32)
        return c

    lax.fori_loop(0, 128, widen, 0)
    toeplitz(w1, big1)
    toeplitz(w2, big2)
    taps[...] = jnp.zeros_like(taps)
    for j in range(9):
        taps[3 * j : 3 * j + 3, :] = sw[j].astype(F32)
    stem_weights(taps[...].astype(BF16), ws)

    lane = lanes_of((16, 128))
    masks = [[lane < STEP * (j + 1) + 16 * h for j in range(5)] for h in range(2)]

    def build(site, slot):
        z0, x0, y0 = corners[0, site], corners[1, site], corners[2, site]
        shift = [lax.rem(STEP * j + 128 - y0, 128) for j in range(6)]
        for u in range(17):
            pieces = []
            for zp in range(2 if u < 16 else 1):
                for kx in range(3):
                    a = vf[z0 + 2 * u + zp, pl.ds(x0 + kx, 8, 4), :]
                    b = vf[z0 + 2 * u + zp, pl.ds(x0 + kx + 2, 8, 4), :]
                    p = jnp.concatenate([a, b], axis=0)
                    pieces.append(pltpu.roll(p.astype(BF16), shift[zp * 3 + kx], 1))
            for h in range(2):
                v = pieces[-1]
                for j in reversed(range(len(pieces) - 1)):
                    v = jnp.where(masks[h][j], pieces[j], v)
                ub[slot, h, u] = v

    bias = jnp.concatenate([sb[...], sb[...]], axis=1)

    def stem(pf, site, slots):
        for h in range(2):
            lhs = jnp.concatenate(
                [
                    jnp.concatenate([ub[t, h, 0:16].reshape(256, 128), ub[t, h, 1:17].reshape(256, 128)], axis=1)
                    for t in slots
                ],
                axis=0,
            )
            for pair in range(2):
                at = (h * 2 + pair) * 256
                r = jnp.dot(lhs, ws[:, at : at + 256], preferred_element_type=F32)
                r = r.reshape(len(slots), 8, 4, 8, 256)
                m = jnp.maximum(jnp.maximum(r[:, :, 0], r[:, :, 1]), jnp.maximum(r[:, :, 2], r[:, :, 3]))
                m = jnp.maximum(m[..., 0:128], m[..., 128:256])
                v = jnp.maximum(m + bias[None, None], 0.0)
                for t in range(len(slots)):
                    for z in range(8):
                        pf[z, h * 2 + pair, pl.ds(site + t, 8, GROUP + 1), :] = v[t, z]

    low = lanes_of((sites, 128)) < 64

    def halo(v, mask):
        r = [pltpu.roll(t, 64, 1) for t in v]
        zero = jnp.zeros_like(r[0])
        return [jnp.where(mask, r[p - 1] if p > 0 else zero, r[p + 1] if p < 3 else zero) for p in range(4)]

    low16 = lanes_of((GROUP, 128)) < 64

    def pack(pf, z, group):
        at = slice(group * GROUP, (group + 1) * GROUP)
        for x in range(8):
            v = [pf[z, p, x * (GROUP + 1) : x * (GROUP + 1) + GROUP, :].astype(BF16) for p in range(4)]
            q = halo(v, low16)
            for p in range(4):
                pq1[z, x, p, at, 0:128] = v[p]
                pq1[z, x, p, at, 128:256] = q[p]

    build(0, 0)
    build(1, 1)
    pfs = (pf0, pf1)
    for group in range(sites // GROUP):
        pf, done = pfs[group % 2], pfs[(group + 1) % 2]

        def four(i, c, group=group, pf=pf, done=done):
            s = group * GROUP + 4 * i
            build(s + 2, 2)
            build(s + 3, 3)
            stem(pf, 4 * i, (0, 1))
            if group > 0:
                pack(done, 2 * i, group - 1)
                pack(done, 2 * i + 1, group - 1)
            build(jnp.minimum(s + 4, sites - 1), 0)
            build(jnp.minimum(s + 5, sites - 1), 1)
            stem(pf, 4 * i + 2, (2, 3))
            return c

        lax.fori_loop(0, GROUP // 4, four, 0)

    def last(z, c):
        pack(pfs[(sites // GROUP - 1) % 2], z, sites // GROUP - 1)
        return c

    lax.fori_loop(0, 8, last, 0)

    def conv(src, big, z, dzs, xb):
        xis = [xi for xi in range(4) if 0 <= 2 * xb - 1 + xi < 8]
        total = None
        for dz in dzs:
            for xi in xis:
                lhs = src[z + dz - 1, 2 * xb - 1 + xi].reshape(4 * sites, 256)
                part = jnp.dot(lhs, big[dz * 4 + xi], preferred_element_type=F32)
                total = part if total is None else total + part
        return total

    bias1 = jnp.concatenate([b1[...]] * 4, axis=1)
    bias2 = jnp.concatenate([b2[...]] * 4, axis=1)

    def first(z, dzs):
        for xb in range(4):
            v = jnp.maximum(conv(pq1, big1, z, dzs, xb) + bias1, 0.0).reshape(4, sites, 256)
            for xo in range(2):
                t = [v[p, :, xo * 128 : xo * 128 + 128].astype(BF16) for p in range(4)]
                q = halo(t, low)
                for p in range(4):
                    pq2[z, 2 * xb + xo, p, :, 0:128] = t[p]
                    pq2[z, 2 * xb + xo, p, :, 128:256] = q[p]

    def second(z, dzs):
        for xb in range(4):
            v = conv(pq2, big2, z, dzs, xb) + bias2
            skip = jnp.concatenate([pq1[z, 2 * xb + xo, :, :, 0:128].reshape(4 * sites, 128) for xo in range(2)], axis=1)
            v = jnp.maximum(v + skip.astype(F32), 0.0).reshape(4, sites, 256)
            acc[...] += jnp.sum(v, axis=0)

    def over_z(step):
        step(0, (1, 2))
        lax.fori_loop(1, 7, lambda z, c: (step(z, (0, 1, 2)), c)[1], 0)
        step(7, (0, 1))

    over_z(first)
    acc[...] = jnp.zeros_like(acc)
    over_z(second)
    a = acc[...]
    mean = (a[:, 0:64] + a[:, 64:128] + a[:, 128:192] + a[:, 192:256]) * (1.0 / 512.0)
    own = jnp.dot(mean, hw[...].astype(F32), precision=lax.Precision.HIGHEST, preferred_element_type=F32) + hb[...]
    half = sites // 2
    out[0:half, :] = jnp.concatenate([own[0:half], own[half:]], axis=1)
    names = jnp.concatenate([dest[...].astype(F32), ids[...].astype(F32)], axis=1)
    out[half : half + 8, :] = jnp.broadcast_to(names, (8, 128))


def embed(volume, corners, destination, svx_ids, stem_w, stem_b, conv_w1, conv_b1, conv_w2, conv_b2, head_w, head_b):
    sites = corners.shape[1]
    sw = stem_w.transpose(0, 1, 3, 2, 4).reshape(9, 3, 64)
    vmem = pl.BlockSpec(memory_space=pltpu.VMEM)
    smem = pl.BlockSpec(memory_space=pltpu.SMEM)
    return pl.pallas_call(
        functools.partial(kernel, sites),
        out_shape=jax.ShapeDtypeStruct((sites // 2 + 8, 128), F32),
        in_specs=[smem] + [vmem] * 11,
        out_specs=vmem,
        scratch_shapes=[
            pltpu.VMEM((128, 128, 128), F32),
            pltpu.VMEM((4, 2, 17, 16, 128), BF16),
            pltpu.VMEM((32, 64), F32),
            pltpu.VMEM((8, 4, 8 * (GROUP + 1), 128), F32),
            pltpu.VMEM((8, 4, 8 * (GROUP + 1), 128), F32),
            pltpu.VMEM((8, 8, 4, sites, 256), BF16),
            pltpu.VMEM((8, 8, 4, sites, 256), BF16),
            pltpu.VMEM((256, 1024), BF16),
            pltpu.VMEM((12, 256, 256), BF16),
            pltpu.VMEM((12, 256, 256), BF16),
            pltpu.VMEM((sites, 256), F32),
        ],
        compiler_params=pltpu.CompilerParams(vmem_limit_bytes=56 * 1024 * 1024),
        cost_estimate=pl.CostEstimate(flops=30_000_000_000, bytes_accessed=6_000_000, transcendentals=0),
    )(
        corners, volume, sw, stem_b.reshape(1, 64), conv_w1.reshape(27, 64, 64), conv_b1.reshape(1, 64),
        conv_w2.reshape(27, 64, 64), conv_b2.reshape(1, 64), head_w, head_b.reshape(1, 64),
        destination.reshape(1, sites), svx_ids.reshape(1, sites),
    )


def collect_kernel(n_xy, own_rows, source_of, me_ref, table, *refs):
    pieces, (batch, sums, hots) = refs[:-3], refs[-3:]
    me = me_ref[0]
    size = pieces[0].shape[0]
    blocks = [(p, r) for p in pieces for r in range(0, size, 40)]
    names = jnp.concatenate([p[r + 32 : r + 33, :] for p, r in blocks], axis=0).astype(jnp.int32)
    dest, ids = names[:, 0:64], names[:, 64:128]
    valid = (dest == me).astype(F32)
    earlier = (lax.broadcasted_iota(jnp.int32, (64, 64), 0) < lax.broadcasted_iota(jnp.int32, (64, 64), 1)).astype(F32)
    rank = jnp.dot(valid, earlier, preferred_element_type=F32).astype(jnp.int32)
    source = jnp.concatenate([jnp.full((1, 64), k, jnp.int32) for k in source_of], axis=0)
    row = jnp.where(dest == me, jnp.bitwise_xor(source, me) * 4 + rank, -1)
    t = table[...]
    want = lax.broadcasted_iota(jnp.int32, (own_rows, 128), 0) + me * own_rows
    found = jnp.zeros((own_rows, 128), jnp.int32)
    lane = lax.broadcasted_iota(jnp.int32, (own_rows, 128), 1)
    for r in range(t.shape[0]):
        found = found + jnp.where(t[r : r + 1, :] == want, lane + r * 128, 0)
    owned = jnp.sum(found, axis=1, keepdims=True)
    rows = lax.broadcasted_iota(jnp.int32, (own_rows, 128), 0)
    for g in range(n_xy // 4):
        for half in range(2):
            cut = slice(half * 32, half * 32 + 32)
            w, s = [jnp.concatenate([x[q : q + 1, cut] for q in range(4 * g, 4 * g + 4)], axis=1) for x in (row, ids)]
            top = half * 2 * own_rows
            at = slice(g * 128, g * 128 + 128)
            hots[top : top + own_rows, at] = (rows == w).astype(F32).astype(BF16)
            hots[top + own_rows : top + 2 * own_rows, at] = (owned == s).astype(F32).astype(BF16)
    total = jnp.zeros((4 * own_rows, 128), F32)
    at = 0
    for p in pieces:
        x = jnp.concatenate([p[r : r + 32, :] for r in range(0, size, 40)], axis=0)
        hi = x.astype(BF16)
        rest = x - hi.astype(F32)
        mid = rest.astype(BF16)
        low = (rest - mid.astype(F32)).astype(BF16)
        parts = jnp.dot(
            hots[:, at : at + x.shape[0]], jnp.concatenate([hi, mid, low], axis=1), preferred_element_type=F32
        )
        total = total + (parts[:, 0:128] + (parts[:, 128:256] + parts[:, 256:384]))
        at += x.shape[0]
    n = own_rows
    both = [total[a : a + n, 0:64] + total[a + 2 * n : a + 3 * n, 64:128] for a in (0, n)]
    turned = jnp.concatenate(both, axis=1).T
    batch[...] = turned[0:64]
    sums[...] = turned[64:128]


def collect(pieces, source_of, table, me, n_xy):
    own_rows = table.size // n_xy
    vmem = pl.BlockSpec(memory_space=pltpu.VMEM)
    return pl.pallas_call(
        functools.partial(collect_kernel, n_xy, own_rows, source_of),
        out_shape=(jax.ShapeDtypeStruct((64, own_rows), F32),) * 2,
        in_specs=[pl.BlockSpec(memory_space=pltpu.SMEM)] + [vmem] * (1 + len(pieces)),
        out_specs=(vmem, vmem),
        scratch_shapes=[pltpu.VMEM((4 * own_rows, n_xy * 32), BF16)],
        compiler_params=pltpu.CompilerParams(vmem_limit_bytes=32 * 1024 * 1024),
    )(me, table, *pieces)


def body(
    volume, corners, destination, svx_ids, svx_rows,
    stem_w, stem_b, conv_w1, conv_b1, conv_w2, conv_b2, head_w, head_b,
):
    n_xy, n_gz = lax.axis_size("xy"), lax.axis_size("gz")

    def swap(a, k, axis="xy", n=n_xy):
        return lax.ppermute(a, axis, [(i, i ^ k) for i in range(n)])

    own = embed(
        volume, corners, destination, svx_ids, stem_w, stem_b, conv_w1, conv_b1, conv_w2, conv_b2, head_w, head_b
    )
    a = jnp.concatenate([own] + [swap(own, k) for k in (2, 4, 6)])
    pieces = [a] + [swap(a, k) for k in (8, 16, 24)]
    pieces = pieces + [swap(p, 1) for p in pieces]
    source_of = [c + x + y for c in (0, 1) for x in (0, 8, 16, 24) for y in (0, 2, 4, 6)]
    me = lax.axis_index("xy").astype(jnp.int32).reshape(1)
    batch, part = collect(pieces, source_of, svx_rows.reshape(-1, 128), me, n_xy)
    z = [part] + [swap(part, k, "gz", n_gz) for k in (1, 2, 3)]
    return ((z[0] + z[1]) + (z[2] + z[3])).T, batch.T


def solution(mesh):
    sites = P(("gz", "xy"))
    placed = (P("gz", "xy", None), P(None, ("gz", "xy")), P(("gz", "xy"), None), sites) + (P(),) * 9
    return jax.shard_map(
        body, mesh=mesh, in_specs=placed, out_specs=(P("xy", None), P(("gz", "xy"), None)), check_vma=False
    )
```

```python
import functools
import jax
import jax.numpy as jnp
from jax import lax
from jax.experimental import pallas as pl
from jax.experimental.pallas import tpu as pltpu
from jax.sharding import PartitionSpec as P

F32, BF16 = jnp.float32, jnp.bfloat16
STEP = 17
GROUP = 16


def lanes_of(shape):
    return lax.broadcasted_iota(jnp.int32, shape, len(shape) - 1)


def toeplitz(w_ref, big_ref):
    zero = jnp.zeros((64, 64), BF16)
    for dz in range(3):
        for xi in range(4):
            for xo in range(2):
                dx = xi - xo
                if 0 <= dx <= 2:
                    w = [w_ref[(dz * 3 + dx) * 3 + dy] for dy in range(3)]
                    rows = [(w[1], w[0]), (w[2], w[1]), (w[0], zero), (zero, w[2])]
                    tile = jnp.concatenate([jnp.concatenate(r, axis=1) for r in rows], axis=0)
                else:
                    tile = jnp.zeros((256, 128), BF16)
                big_ref[dz * 4 + xi, :, xo * 128 : (xo + 1) * 128] = tile


def stem_weights(taps, ws_ref):
    t = lax.broadcasted_iota(jnp.int32, (256, 32), 1)
    k = lax.broadcasted_iota(jnp.int32, (256, 32), 0)
    kz, kx, ky = t // 9, (t // 3) % 3, t % 3
    base = jnp.where(kz == 2, 128 + STEP * kx, STEP * (kz * 3 + kx)) + ky
    base = jnp.where(t < 27, base, -1000)
    for pair in range(4):
        for par in range(2):
            cols = []
            for inner in range(2):
                sy = 4 * pair + 2 * inner + par
                hot = (k == base + 2 * sy).astype(F32).astype(BF16)
                cols.append(jnp.dot(hot, taps, preferred_element_type=F32).astype(BF16))
            at = (pair * 2 + par) * 128
            ws_ref[:, at : at + 128] = jnp.concatenate(cols, axis=1)


def kernel(sites, corners, vol, sw, sb, w1, b1, w2, b2, hw, hb, dest, ids, out, vf, ub, taps, pf0, pf1, pq1, pq2, ws, big1, big2, acc, vb, wa, wb, sems):
    copies = [
        pltpu.make_async_copy(vol.at[pl.ds(16 * c, 16)], vb.at[pl.ds(16 * c, 16)], sems.at[c]) for c in range(8)
    ]
    copies += [pltpu.make_async_copy(w1, wa, sems.at[8]), pltpu.make_async_copy(w2, wb, sems.at[9])]
    for copy in copies:
        copy.start()
    taps[...] = jnp.zeros_like(taps)
    for j in range(9):
        taps[3 * j : 3 * j + 3, :] = sw[j].astype(F32)
    stem_weights(taps[...].astype(BF16), ws)
    for c in range(8):
        copies[c].wait()

        def widen(i, carry, c=c):
            for k in range(8):
                z = 16 * c + 8 * i + k
                vf[z] = vb[z].astype(F32)
            return carry

        lax.fori_loop(0, 2, widen, 0)
    copies[8].wait()
    toeplitz(wa, big1)
    copies[9].wait()
    toeplitz(wb, big2)

    lane = lanes_of((16, 128))
    masks = [[lane < STEP * (j + 1) + 16 * h for j in range(5)] for h in range(2)]

    def build(site, slot):
        z0, x0, y0 = corners[0, site], corners[1, site], corners[2, site]
        shift = [lax.rem(STEP * j + 128 - y0, 128) for j in range(6)]
        for u in range(17):
            pieces = []
            for zp in range(2 if u < 16 else 1):
                for kx in range(3):
                    a = vf[z0 + 2 * u + zp, pl.ds(x0 + kx, 8, 4), :]
                    b = vf[z0 + 2 * u + zp, pl.ds(x0 + kx + 2, 8, 4), :]
                    p = jnp.concatenate([a, b], axis=0)
                    pieces.append(pltpu.roll(p.astype(BF16), shift[zp * 3 + kx], 1))
            for h in range(2):
                v = pieces[-1]
                for j in reversed(range(len(pieces) - 1)):
                    v = jnp.where(masks[h][j], pieces[j], v)
                ub[slot, h, u] = v

    bias = jnp.concatenate([sb[...], sb[...]], axis=1)

    def stem(pf, site, slots):
        for h in range(2):
            lhs = jnp.concatenate(
                [
                    jnp.concatenate([ub[t, h, 0:16].reshape(256, 128), ub[t, h, 1:17].reshape(256, 128)], axis=1)
                    for t in slots
                ],
                axis=0,
            )
            for pair in range(2):
                at = (h * 2 + pair) * 256
                r = jnp.dot(lhs, ws[:, at : at + 256], preferred_element_type=F32)
                r = r.reshape(len(slots), 8, 4, 8, 256)
                m = jnp.maximum(jnp.maximum(r[:, :, 0], r[:, :, 1]), jnp.maximum(r[:, :, 2], r[:, :, 3]))
                m = jnp.maximum(m[..., 0:128], m[..., 128:256])
                v = jnp.maximum(m + bias[None, None], 0.0)
                for t in range(len(slots)):
                    for z in range(8):
                        pf[z, h * 2 + pair, pl.ds(site + t, 8, GROUP + 1), :] = v[t, z]

    low = lanes_of((sites, 128)) < 64

    def halo(v, mask):
        r = [pltpu.roll(t, 64, 1) for t in v]
        zero = jnp.zeros_like(r[0])
        return [jnp.where(mask, r[p - 1] if p > 0 else zero, r[p + 1] if p < 3 else zero) for p in range(4)]

    low16 = lanes_of((GROUP, 128)) < 64

    def pack(pf, z, group):
        at = slice(group * GROUP, (group + 1) * GROUP)
        for x in range(8):
            v = [pf[z, p, x * (GROUP + 1) : x * (GROUP + 1) + GROUP, :].astype(BF16) for p in range(4)]
            q = halo(v, low16)
            for p in range(4):
                pq1[z, x, p, at, 0:128] = v[p]
                pq1[z, x, p, at, 128:256] = q[p]

    for t in range(4):
        build(t, t)
    pfs = (pf0, pf1)
    for group in range(sites // GROUP):
        pf, done = pfs[group % 2], pfs[(group + 1) % 2]

        def eight(i, c, group=group, pf=pf, done=done):
            s = group * GROUP + 8 * i
            for part in range(2):
                for t in range(4):
                    build(jnp.minimum(s + 4 * part + 4 + t, sites - 1), 4 * (1 - part) + t)
                for t in (0, 2):
                    stem(pf, 8 * i + 4 * part + t, (4 * part + t, 4 * part + t + 1))
                if group > 0:
                    for z in range(2):
                        pack(done, 4 * i + 2 * part + z, group - 1)
            return c

        lax.fori_loop(0, GROUP // 8, eight, 0)

    def last(z, c):
        pack(pfs[(sites // GROUP - 1) % 2], z, sites // GROUP - 1)
        return c

    for z in range(8):
        last(z, 0)

    def conv(src, big, z, dzs, xb, nz):
        xis = [xi for xi in range(4) if 0 <= 2 * xb - 1 + xi < 8]
        total = None
        for dz in dzs:
            for xi in xis:
                lhs = src[pl.ds(z + dz - 1, nz), 2 * xb - 1 + xi].reshape(nz * 4 * sites, 256)
                part = jnp.dot(lhs, big[dz * 4 + xi], preferred_element_type=F32)
                total = part if total is None else total + part
        return total

    bias1 = jnp.concatenate([b1[...]] * 4, axis=1)
    bias2 = jnp.concatenate([b2[...]] * 4, axis=1)

    def first(z, dzs, nz):
        for xb in range(4):
            v = jnp.maximum(conv(pq1, big1, z, dzs, xb, nz) + bias1, 0.0).reshape(nz, 4, sites, 256)
            for k in range(nz):
                for xo in range(2):
                    t = [v[k, p, :, xo * 128 : xo * 128 + 128].astype(BF16) for p in range(4)]
                    q = halo(t, low)
                    for p in range(4):
                        pq2[z + k, 2 * xb + xo, p, :, 0:128] = t[p]
                        pq2[z + k, 2 * xb + xo, p, :, 128:256] = q[p]

    def second(z, dzs, nz):
        for xb in range(4):
            v = conv(pq2, big2, z, dzs, xb, nz) + bias2
            skip = jnp.concatenate(
                [pq1[pl.ds(z, nz), 2 * xb + xo, :, :, 0:128].reshape(nz * 4 * sites, 128) for xo in range(2)], axis=1
            )
            v = jnp.maximum(v + skip.astype(F32), 0.0).reshape(nz * 4, sites, 256)
            acc[...] += jnp.sum(v, axis=0)

    def over_z(step):
        step(0, (1, 2), 1)
        step(1, (0, 1, 2), 3)
        step(4, (0, 1, 2), 3)
        step(7, (0, 1), 1)

    over_z(first)
    acc[...] = jnp.zeros_like(acc)
    over_z(second)
    a = acc[...]
    mean = (a[:, 0:64] + a[:, 64:128] + a[:, 128:192] + a[:, 192:256]) * (1.0 / 512.0)
    own = jnp.dot(mean, hw[...].astype(F32), precision=lax.Precision.HIGHEST, preferred_element_type=F32) + hb[...]
    half = sites // 2
    out[0:half, :] = jnp.concatenate([own[0:half], own[half:]], axis=1)
    names = jnp.concatenate([dest[...].astype(F32), ids[...].astype(F32)], axis=1)
    out[half : half + 8, :] = jnp.broadcast_to(names, (8, 128))


def embed(volume, corners, destination, svx_ids, stem_w, stem_b, conv_w1, conv_b1, conv_w2, conv_b2, head_w, head_b):
    sites = corners.shape[1]
    sw = stem_w.transpose(0, 1, 3, 2, 4).reshape(9, 3, 64)
    vmem = pl.BlockSpec(memory_space=pltpu.VMEM)
    hbm = pl.BlockSpec(memory_space=pl.ANY)
    smem = pl.BlockSpec(memory_space=pltpu.SMEM)
    return pl.pallas_call(
        functools.partial(kernel, sites),
        out_shape=jax.ShapeDtypeStruct((sites // 2 + 8, 128), F32),
        in_specs=[smem, hbm, vmem, vmem, hbm, vmem, hbm] + [vmem] * 5,
        out_specs=vmem,
        scratch_shapes=[
            pltpu.VMEM((128, 128, 128), F32),
            pltpu.VMEM((8, 2, 17, 16, 128), BF16),
            pltpu.VMEM((32, 64), F32),
            pltpu.VMEM((8, 4, 8 * (GROUP + 1), 128), F32),
            pltpu.VMEM((8, 4, 8 * (GROUP + 1), 128), F32),
            pltpu.VMEM((8, 8, 4, sites, 256), BF16),
            pltpu.VMEM((8, 8, 4, sites, 256), BF16),
            pltpu.VMEM((256, 1024), BF16),
            pltpu.VMEM((12, 256, 256), BF16),
            pltpu.VMEM((12, 256, 256), BF16),
            pltpu.VMEM((sites, 256), F32),
            pltpu.VMEM((128, 128, 128), BF16),
            pltpu.VMEM((27, 64, 64), BF16),
            pltpu.VMEM((27, 64, 64), BF16),
            pltpu.SemaphoreType.DMA((10,)),
        ],
        compiler_params=pltpu.CompilerParams(vmem_limit_bytes=60 * 1024 * 1024),
        cost_estimate=pl.CostEstimate(flops=30_000_000_000, bytes_accessed=6_000_000, transcendentals=0),
    )(
        corners, volume, sw, stem_b.reshape(1, 64), conv_w1.reshape(27, 64, 64), conv_b1.reshape(1, 64),
        conv_w2.reshape(27, 64, 64), conv_b2.reshape(1, 64), head_w, head_b.reshape(1, 64),
        destination.reshape(1, sites), svx_ids.reshape(1, sites),
    )


def collect_kernel(n_xy, own_rows, source_of, me_ref, table, *refs):
    pieces, (batch, sums, hots) = refs[:-3], refs[-3:]
    me = me_ref[0]
    size = pieces[0].shape[0]
    blocks = [(p, r) for p in pieces for r in range(0, size, 40)]
    names = jnp.concatenate([p[r + 32 : r + 33, :] for p, r in blocks], axis=0).astype(jnp.int32)
    dest, ids = names[:, 0:64], names[:, 64:128]
    valid = (dest == me).astype(F32)
    earlier = (lax.broadcasted_iota(jnp.int32, (64, 64), 0) < lax.broadcasted_iota(jnp.int32, (64, 64), 1)).astype(F32)
    rank = jnp.dot(valid, earlier, preferred_element_type=F32).astype(jnp.int32)
    source = jnp.concatenate([jnp.full((1, 64), k, jnp.int32) for k in source_of], axis=0)
    row = jnp.where(dest == me, jnp.bitwise_xor(source, me) * 4 + rank, -1)
    t = table[...]
    want = lax.broadcasted_iota(jnp.int32, (own_rows, 128), 0) + me * own_rows
    found = jnp.zeros((own_rows, 128), jnp.int32)
    lane = lax.broadcasted_iota(jnp.int32, (own_rows, 128), 1)
    for r in range(t.shape[0]):
        found = found + jnp.where(t[r : r + 1, :] == want, lane + r * 128, 0)
    owned = jnp.sum(found, axis=1, keepdims=True)
    rows = lax.broadcasted_iota(jnp.int32, (own_rows, 128), 0)
    for g in range(n_xy // 4):
        for half in range(2):
            cut = slice(half * 32, half * 32 + 32)
            w, s = [jnp.concatenate([x[q : q + 1, cut] for q in range(4 * g, 4 * g + 4)], axis=1) for x in (row, ids)]
            top = half * 2 * own_rows
            at = slice(g * 128, g * 128 + 128)
            hots[top : top + own_rows, at] = (rows == w).astype(F32).astype(BF16)
            hots[top + own_rows : top + 2 * own_rows, at] = (owned == s).astype(F32).astype(BF16)
    total = jnp.zeros((4 * own_rows, 128), F32)
    at = 0
    for p in pieces:
        x = jnp.concatenate([p[r : r + 32, :] for r in range(0, size, 40)], axis=0)
        hi = x.astype(BF16)
        rest = x - hi.astype(F32)
        mid = rest.astype(BF16)
        low = (rest - mid.astype(F32)).astype(BF16)
        parts = jnp.dot(
            hots[:, at : at + x.shape[0]], jnp.concatenate([hi, mid, low], axis=1), preferred_element_type=F32
        )
        total = total + (parts[:, 0:128] + (parts[:, 128:256] + parts[:, 256:384]))
        at += x.shape[0]
    n = own_rows
    both = [total[a : a + n, 0:64] + total[a + 2 * n : a + 3 * n, 64:128] for a in (0, n)]
    turned = jnp.concatenate(both, axis=1).T
    batch[...] = turned[0:64]
    sums[...] = turned[64:128]


def collect(pieces, source_of, table, me, n_xy):
    own_rows = table.size // n_xy
    vmem = pl.BlockSpec(memory_space=pltpu.VMEM)
    return pl.pallas_call(
        functools.partial(collect_kernel, n_xy, own_rows, source_of),
        out_shape=(jax.ShapeDtypeStruct((64, own_rows), F32),) * 2,
        in_specs=[pl.BlockSpec(memory_space=pltpu.SMEM)] + [vmem] * (1 + len(pieces)),
        out_specs=(vmem, vmem),
        scratch_shapes=[pltpu.VMEM((4 * own_rows, n_xy * 32), BF16)],
        compiler_params=pltpu.CompilerParams(vmem_limit_bytes=32 * 1024 * 1024),
    )(me, table, *pieces)


def body(
    volume, corners, destination, svx_ids, svx_rows,
    stem_w, stem_b, conv_w1, conv_b1, conv_w2, conv_b2, head_w, head_b,
):
    n_xy, n_gz = lax.axis_size("xy"), lax.axis_size("gz")

    def swap(a, k, axis="xy", n=n_xy):
        return lax.ppermute(a, axis, [(i, i ^ k) for i in range(n)])

    own = embed(
        volume, corners, destination, svx_ids, stem_w, stem_b, conv_w1, conv_b1, conv_w2, conv_b2, head_w, head_b
    )
    a = jnp.concatenate([own] + [swap(own, k) for k in (2, 4, 6)])
    pieces = [a] + [swap(a, k) for k in (8, 16, 24)]
    pieces = pieces + [swap(p, 1) for p in pieces]
    source_of = [c + x + y for c in (0, 1) for x in (0, 8, 16, 24) for y in (0, 2, 4, 6)]
    me = lax.axis_index("xy").astype(jnp.int32).reshape(1)
    batch, part = collect(pieces, source_of, svx_rows.reshape(-1, 128), me, n_xy)
    z = [part] + [swap(part, k, "gz", n_gz) for k in (1, 2, 3)]
    return ((z[0] + z[1]) + (z[2] + z[3])).T, batch.T


def solution(mesh):
    sites = P(("gz", "xy"))
    placed = (P("gz", "xy", None), P(None, ("gz", "xy")), P(("gz", "xy"), None), sites) + (P(),) * 9
    return jax.shard_map(
        body, mesh=mesh, in_specs=placed, out_specs=(P("xy", None), P(("gz", "xy"), None)), check_vma=False
    )
```

```python
import functools
import jax
import jax.numpy as jnp
from jax import lax
from jax.experimental import pallas as pl
from jax.experimental.pallas import tpu as pltpu
from jax.sharding import PartitionSpec as P

F32, BF16 = jnp.float32, jnp.bfloat16
STEP = 17
GROUP = 16


def lanes_of(shape):
    return lax.broadcasted_iota(jnp.int32, shape, len(shape) - 1)


def toeplitz(w_ref, big_ref):
    zero = jnp.zeros((64, 64), BF16)
    for dz in range(3):
        for xi in range(4):
            for xo in range(2):
                dx = xi - xo
                if 0 <= dx <= 2:
                    w = [w_ref[(dz * 3 + dx) * 3 + dy] for dy in range(3)]
                    rows = [(w[1], w[0]), (w[2], w[1]), (w[0], zero), (zero, w[2])]
                    tile = jnp.concatenate([jnp.concatenate(r, axis=1) for r in rows], axis=0)
                else:
                    tile = jnp.zeros((256, 128), BF16)
                big_ref[dz * 4 + xi, :, xo * 128 : (xo + 1) * 128] = tile


def owned_ids(table, me, rows):
    want = lax.broadcasted_iota(jnp.int32, (rows, 128), 0) + me * rows
    lane = lanes_of((rows, 128))
    found = jnp.zeros((rows, 128), jnp.int32)
    for r in range(table.shape[0]):
        found = found + jnp.where(table[r : r + 1, :] == want, lane + r * 128, 0)
    return jnp.broadcast_to(jnp.sum(found, axis=1, keepdims=True), (rows, 128))


def stem_weights(taps, ws_ref):
    t = lax.broadcasted_iota(jnp.int32, (256, 32), 1)
    k = lax.broadcasted_iota(jnp.int32, (256, 32), 0)
    kz, kx, ky = t // 9, (t // 3) % 3, t % 3
    base = jnp.where(kz == 2, 128 + STEP * kx, STEP * (kz * 3 + kx)) + ky
    base = jnp.where(t < 27, base, -1000)
    for pair in range(4):
        for par in range(2):
            cols = []
            for inner in range(2):
                sy = 4 * pair + 2 * inner + par
                hot = (k == base + 2 * sy).astype(F32).astype(BF16)
                cols.append(jnp.dot(hot, taps, preferred_element_type=F32).astype(BF16))
            at = (pair * 2 + par) * 128
            ws_ref[:, at : at + 128] = jnp.concatenate(cols, axis=1)


def kernel(sites, corners, vol, sw, sb, w1, b1, w2, b2, hw, hb, dest, ids, me_ref, table, out, owned, vf, ub, taps, pf0, pf1, pq1, pq2, ws, big1, big2, acc, vb, wa, wb, sems):
    copies = [
        pltpu.make_async_copy(vol.at[pl.ds(16 * c, 16)], vb.at[pl.ds(16 * c, 16)], sems.at[c]) for c in range(8)
    ]
    copies += [pltpu.make_async_copy(w1, wa, sems.at[8]), pltpu.make_async_copy(w2, wb, sems.at[9])]
    for copy in copies:
        copy.start()
    owned[...] = owned_ids(table[...], me_ref[0], owned.shape[0])
    taps[...] = jnp.zeros_like(taps)
    for j in range(9):
        taps[3 * j : 3 * j + 3, :] = sw[j].astype(F32)
    stem_weights(taps[...].astype(BF16), ws)
    for c in range(8):
        copies[c].wait()

        def widen(i, carry, c=c):
            for k in range(8):
                z = 16 * c + 8 * i + k
                vf[z, 0:128, :] = vb[z].astype(F32)
            return carry

        lax.fori_loop(0, 2, widen, 0)
    copies[8].wait()
    toeplitz(wa, big1)
    copies[9].wait()
    toeplitz(wb, big2)

    lane = lanes_of((16, 128))
    masks = [[lane < STEP * (j + 1) + 16 * h for j in range(5)] for h in range(2)]

    def build(site, slot):
        z0, x0, y0 = corners[0, site], corners[1, site], corners[2, site]
        shift = [lax.rem(STEP * j + 128 - y0, 128) for j in range(6)]
        for u in range(17):
            pieces = []
            for zp in range(2 if u < 16 else 1):
                for kx in range(3):
                    a = vf[z0 + 2 * u + zp, pl.ds(x0 + kx, 8, 4), :]
                    b = vf[z0 + 2 * u + zp, pl.ds(x0 + kx + 2, 8, 4), :]
                    p = jnp.concatenate([a, b], axis=0)
                    pieces.append(pltpu.roll(p.astype(BF16), shift[zp * 3 + kx], 1))
            for h in range(2):
                v = pieces[-1]
                for j in reversed(range(len(pieces) - 1)):
                    v = jnp.where(masks[h][j], pieces[j], v)
                ub[slot, h, u] = v

    bias = jnp.concatenate([sb[...], sb[...]], axis=1)

    def stem(pf, site, slots):
        for h in range(2):
            lhs = jnp.concatenate(
                [
                    jnp.concatenate([ub[t, h, 0:16].reshape(256, 128), ub[t, h, 1:17].reshape(256, 128)], axis=1)
                    for t in slots
                ],
                axis=0,
            )
            for pair in range(2):
                at = (h * 2 + pair) * 256
                r = jnp.dot(lhs, ws[:, at : at + 256], preferred_element_type=F32)
                r = r.reshape(len(slots), 8, 4, 8, 256)
                m = jnp.maximum(jnp.maximum(r[:, :, 0], r[:, :, 1]), jnp.maximum(r[:, :, 2], r[:, :, 3]))
                m = jnp.maximum(m[..., 0:128], m[..., 128:256])
                v = jnp.maximum(m + bias[None, None], 0.0)
                for t in range(len(slots)):
                    for z in range(8):
                        pf[z, h * 2 + pair, pl.ds(site + t, 8, GROUP + 1), :] = v[t, z]

    low = lanes_of((sites, 128)) < 64

    def halo(v, mask):
        r = [pltpu.roll(t, 64, 1) for t in v]
        zero = jnp.zeros_like(r[0])
        return [jnp.where(mask, r[p - 1] if p > 0 else zero, r[p + 1] if p < 3 else zero) for p in range(4)]

    low16 = lanes_of((GROUP, 128)) < 64

    def pack(pf, z, group):
        at = slice(group * GROUP, (group + 1) * GROUP)
        for x in range(8):
            v = [pf[z, p, x * (GROUP + 1) : x * (GROUP + 1) + GROUP, :].astype(BF16) for p in range(4)]
            q = halo(v, low16)
            for p in range(4):
                pq1[z, x, p, at, 0:128] = v[p]
                pq1[z, x, p, at, 128:256] = q[p]

    for t in range(4):
        build(t, t)
    pfs = (pf0, pf1)
    for group in range(sites // GROUP):
        pf, done = pfs[group % 2], pfs[(group + 1) % 2]

        def eight(i, c, group=group, pf=pf, done=done):
            s = group * GROUP + 8 * i
            for part in range(2):
                for t in range(4):
                    build(jnp.minimum(s + 4 * part + 4 + t, sites - 1), 4 * (1 - part) + t)
                for t in (0, 2):
                    stem(pf, 8 * i + 4 * part + t, (4 * part + t, 4 * part + t + 1))
                if group > 0:
                    for z in range(2):
                        pack(done, 4 * i + 2 * part + z, group - 1)
            return c

        lax.fori_loop(0, GROUP // 8, eight, 0)

    def last(z, c):
        pack(pfs[(sites // GROUP - 1) % 2], z, sites // GROUP - 1)
        return c

    for z in range(8):
        last(z, 0)

    def conv(src, big, z, dzs, xb, nz):
        xis = [xi for xi in range(4) if 0 <= 2 * xb - 1 + xi < 8]
        total = None
        for dz in dzs:
            for xi in xis:
                lhs = src[pl.ds(z + dz - 1, nz), 2 * xb - 1 + xi].reshape(nz * 4 * sites, 256)
                part = jnp.dot(lhs, big[dz * 4 + xi], preferred_element_type=F32)
                total = part if total is None else total + part
        return total

    bias1 = jnp.concatenate([b1[...]] * 4, axis=1)
    bias2 = jnp.concatenate([b2[...]] * 4, axis=1)

    def first(z, dzs, nz):
        for xb in range(4):
            v = jnp.maximum(conv(pq1, big1, z, dzs, xb, nz) + bias1, 0.0).reshape(nz, 4, sites, 256)
            for k in range(nz):
                for xo in range(2):
                    t = [v[k, p, :, xo * 128 : xo * 128 + 128].astype(BF16) for p in range(4)]
                    q = halo(t, low)
                    for p in range(4):
                        pq2[z + k, 2 * xb + xo, p, :, 0:128] = t[p]
                        pq2[z + k, 2 * xb + xo, p, :, 128:256] = q[p]

    def second(z, dzs, nz):
        for xb in range(4):
            v = conv(pq2, big2, z, dzs, xb, nz) + bias2
            skip = jnp.concatenate(
                [pq1[pl.ds(z, nz), 2 * xb + xo, :, :, 0:128].reshape(nz * 4 * sites, 128) for xo in range(2)], axis=1
            )
            v = jnp.maximum(v + skip.astype(F32), 0.0).reshape(nz * 4, sites, 256)
            acc[...] += jnp.sum(v, axis=0)

    def over_z(step):
        step(0, (1, 2), 1)
        step(1, (0, 1, 2), 3)
        step(4, (0, 1, 2), 3)
        step(7, (0, 1), 1)

    over_z(first)
    acc[...] = jnp.zeros_like(acc)
    over_z(second)
    a = acc[...]
    mean = (a[:, 0:64] + a[:, 64:128] + a[:, 128:192] + a[:, 192:256]) * (1.0 / 512.0)
    own = jnp.dot(mean, hw[...].astype(F32), precision=lax.Precision.HIGHEST, preferred_element_type=F32) + hb[...]
    half = sites // 2
    out[0:half, :] = jnp.concatenate([own[0:half], own[half:]], axis=1)
    names = jnp.concatenate([dest[...].astype(F32), ids[...].astype(F32)], axis=1)
    out[half : half + 8, :] = jnp.broadcast_to(names, (8, 128))


def embed(me, table, own_rows, volume, corners, destination, svx_ids, stem_w, stem_b, conv_w1, conv_b1, conv_w2, conv_b2, head_w, head_b):
    sites = corners.shape[1]
    sw = stem_w.transpose(0, 1, 3, 2, 4).reshape(9, 3, 64)
    vmem = pl.BlockSpec(memory_space=pltpu.VMEM)
    hbm = pl.BlockSpec(memory_space=pl.ANY)
    smem = pl.BlockSpec(memory_space=pltpu.SMEM)
    return pl.pallas_call(
        functools.partial(kernel, sites),
        out_shape=(
            jax.ShapeDtypeStruct((sites // 2 + 8, 128), F32),
            jax.ShapeDtypeStruct((own_rows, 128), jnp.int32),
        ),
        in_specs=[smem, hbm, vmem, vmem, hbm, vmem, hbm] + [vmem] * 5 + [smem, vmem],
        out_specs=(vmem, vmem),
        scratch_shapes=[
            pltpu.VMEM((128, 136, 128), F32),
            pltpu.VMEM((8, 2, 17, 16, 128), BF16),
            pltpu.VMEM((32, 64), F32),
            pltpu.VMEM((8, 4, 8 * (GROUP + 1) + GROUP, 128), F32),
            pltpu.VMEM((8, 4, 8 * (GROUP + 1) + GROUP, 128), F32),
            pltpu.VMEM((8, 8, 4, sites, 256), BF16),
            pltpu.VMEM((8, 8, 4, sites, 256), BF16),
            pltpu.VMEM((256, 1024), BF16),
            pltpu.VMEM((12, 256, 256), BF16),
            pltpu.VMEM((12, 256, 256), BF16),
            pltpu.VMEM((sites, 256), F32),
            pltpu.VMEM((128, 128, 128), BF16),
            pltpu.VMEM((27, 64, 64), BF16),
            pltpu.VMEM((27, 64, 64), BF16),
            pltpu.SemaphoreType.DMA((10,)),
        ],
        compiler_params=pltpu.CompilerParams(vmem_limit_bytes=60 * 1024 * 1024),
        cost_estimate=pl.CostEstimate(flops=30_000_000_000, bytes_accessed=6_000_000, transcendentals=0),
    )(
        corners, volume, sw, stem_b.reshape(1, 64), conv_w1.reshape(27, 64, 64), conv_b1.reshape(1, 64),
        conv_w2.reshape(27, 64, 64), conv_b2.reshape(1, 64), head_w, head_b.reshape(1, 64),
        destination.reshape(1, sites), svx_ids.reshape(1, sites), me, table,
    )


def collect_kernel(n_xy, own_rows, source_of, me_ref, owned_ref, *refs):
    pieces, (batch, sums, hots) = refs[:-3], refs[-3:]
    me = me_ref[0]
    size = pieces[0].shape[0]
    blocks = [(p, r) for p in pieces for r in range(0, size, 40)]
    names = jnp.concatenate([p[r + 32 : r + 33, :] for p, r in blocks], axis=0).astype(jnp.int32)
    dest, ids = names[:, 0:64], names[:, 64:128]
    valid = (dest == me).astype(F32)
    earlier = (lax.broadcasted_iota(jnp.int32, (64, 64), 0) < lax.broadcasted_iota(jnp.int32, (64, 64), 1)).astype(F32)
    rank = jnp.dot(valid, earlier, preferred_element_type=F32).astype(jnp.int32)
    source = jnp.concatenate([jnp.full((1, 64), k, jnp.int32) for k in source_of], axis=0)
    row = jnp.where(dest == me, jnp.bitwise_xor(source, me) * 4 + rank, -1)
    owned = owned_ref[...]
    rows = lax.broadcasted_iota(jnp.int32, (own_rows, 128), 0)
    for g in range(n_xy // 4):
        for half in range(2):
            cut = slice(half * 32, half * 32 + 32)
            w, s = [jnp.concatenate([x[q : q + 1, cut] for q in range(4 * g, 4 * g + 4)], axis=1) for x in (row, ids)]
            top = half * 2 * own_rows
            at = slice(g * 128, g * 128 + 128)
            hots[top : top + own_rows, at] = (rows == w).astype(F32).astype(BF16)
            hots[top + own_rows : top + 2 * own_rows, at] = (owned == s).astype(F32).astype(BF16)
    x = jnp.concatenate([p[r : r + 32, :] for p, r in blocks], axis=0)
    hi = x.astype(BF16)
    rest = x - hi.astype(F32)
    mid = rest.astype(BF16)
    low = (rest - mid.astype(F32)).astype(BF16)
    total = jnp.dot(hots[...], jnp.concatenate([hi, mid, low], axis=1), preferred_element_type=F32)
    total = total[:, 0:128] + (total[:, 128:256] + total[:, 256:384])
    n = own_rows
    both = [total[a : a + n, 0:64] + total[a + 2 * n : a + 3 * n, 64:128] for a in (0, n)]
    turned = jnp.concatenate(both, axis=1).T
    batch[...] = turned[0:64]
    sums[...] = turned[64:128]


def collect(pieces, source_of, owned, me, n_xy):
    own_rows = owned.shape[0]
    vmem = pl.BlockSpec(memory_space=pltpu.VMEM)
    return pl.pallas_call(
        functools.partial(collect_kernel, n_xy, own_rows, source_of),
        out_shape=(jax.ShapeDtypeStruct((64, own_rows), F32),) * 2,
        in_specs=[pl.BlockSpec(memory_space=pltpu.SMEM)] + [vmem] * (1 + len(pieces)),
        out_specs=(vmem, vmem),
        scratch_shapes=[pltpu.VMEM((4 * own_rows, n_xy * 32), BF16)],
        compiler_params=pltpu.CompilerParams(vmem_limit_bytes=32 * 1024 * 1024),
    )(me, owned, *pieces)


def body(
    volume, corners, destination, svx_ids, svx_rows,
    stem_w, stem_b, conv_w1, conv_b1, conv_w2, conv_b2, head_w, head_b,
):
    n_xy, n_gz = lax.axis_size("xy"), lax.axis_size("gz")

    def swap(a, k, axis="xy", n=n_xy):
        return lax.ppermute(a, axis, [(i, i ^ k) for i in range(n)])

    me = lax.axis_index("xy").astype(jnp.int32).reshape(1)
    own, owned = embed(
        me, svx_rows.reshape(-1, 128), svx_rows.size // n_xy, volume, corners, destination, svx_ids, stem_w, stem_b, conv_w1, conv_b1, conv_w2, conv_b2, head_w, head_b
    )
    a = jnp.concatenate([own] + [swap(own, k) for k in (2, 4, 6)])
    pieces = [a] + [swap(a, k) for k in (8, 16, 24)]
    pieces = pieces + [swap(p, 1) for p in pieces]
    source_of = [c + x + y for c in (0, 1) for x in (0, 8, 16, 24) for y in (0, 2, 4, 6)]
    batch, part = collect(pieces, source_of, owned, me, n_xy)
    z = [part] + [swap(part, k, "gz", n_gz) for k in (1, 2, 3)]
    return ((z[0] + z[1]) + (z[2] + z[3])).T, batch.T


def solution(mesh):
    sites = P(("gz", "xy"))
    placed = (P("gz", "xy", None), P(None, ("gz", "xy")), P(("gz", "xy"), None), sites) + (P(),) * 9
    return jax.shard_map(
        body, mesh=mesh, in_specs=placed, out_specs=(P("xy", None), P(("gz", "xy"), None)), check_vma=False
    )
```

```python
import functools
import jax
import jax.numpy as jnp
from jax import lax
from jax.experimental import pallas as pl
from jax.experimental.pallas import tpu as pltpu
from jax.sharding import PartitionSpec as P

F32, BF16 = jnp.float32, jnp.bfloat16
STEP = 17
GROUP = 16


def lanes_of(shape):
    return lax.broadcasted_iota(jnp.int32, shape, len(shape) - 1)


def toeplitz(w_ref, big_ref):
    zero = jnp.zeros((64, 64), BF16)
    for dz in range(3):
        for xi in range(4):
            for xo in range(2):
                dx = xi - xo
                if 0 <= dx <= 2:
                    w = [w_ref[(dz * 3 + dx) * 3 + dy] for dy in range(3)]
                    rows = [(w[1], w[0]), (w[2], w[1]), (w[0], zero), (zero, w[2])]
                    tile = jnp.concatenate([jnp.concatenate(r, axis=1) for r in rows], axis=0)
                else:
                    tile = jnp.zeros((256, 128), BF16)
                big_ref[dz * 4 + xi, :, xo * 128 : (xo + 1) * 128] = tile


def stem_weights(taps, ws_ref):
    t = lax.broadcasted_iota(jnp.int32, (256, 32), 1)
    k = lax.broadcasted_iota(jnp.int32, (256, 32), 0)
    kz, kx, ky = t // 9, (t // 3) % 3, t % 3
    base = jnp.where(kz == 2, 128 + STEP * kx, STEP * (kz * 3 + kx)) + ky
    base = jnp.where(t < 27, base, -1000)
    for pair in range(4):
        for par in range(2):
            cols = []
            for inner in range(2):
                sy = 4 * pair + 2 * inner + par
                hot = (k == base + 2 * sy).astype(F32).astype(BF16)
                cols.append(jnp.dot(hot, taps, preferred_element_type=F32).astype(BF16))
            at = (pair * 2 + par) * 128
            ws_ref[:, at : at + 128] = jnp.concatenate(cols, axis=1)


def kernel(sites, corners, vol, sw, sb, w1, b1, w2, b2, hw, hb, dest, ids, out, vf, ub, taps, pf0, pf1, pq1, pq2, ws, big1, big2, acc, vb, wa, wb, sems):
    copies = [
        pltpu.make_async_copy(vol.at[pl.ds(16 * c, 16)], vb.at[pl.ds(16 * c, 16)], sems.at[c]) for c in range(8)
    ]
    copies += [pltpu.make_async_copy(w1, wa, sems.at[8]), pltpu.make_async_copy(w2, wb, sems.at[9])]
    for copy in copies:
        copy.start()
    taps[...] = jnp.zeros_like(taps)
    for j in range(9):
        taps[3 * j : 3 * j + 3, :] = sw[j].astype(F32)
    stem_weights(taps[...].astype(BF16), ws)
    for c in range(8):
        copies[c].wait()

        def widen(i, carry, c=c):
            for k in range(8):
                z = 16 * c + 8 * i + k
                vf[z, 0:128, :] = vb[z].astype(F32)
            return carry

        lax.fori_loop(0, 2, widen, 0)
    copies[8].wait()
    toeplitz(wa, big1)
    copies[9].wait()
    toeplitz(wb, big2)

    lane = lanes_of((16, 128))
    masks = [[lane < STEP * (j + 1) + 16 * h for j in range(5)] for h in range(2)]

    def build(site, slot):
        z0, x0, y0 = corners[0, site], corners[1, site], corners[2, site]
        shift = [lax.rem(STEP * j + 128 - y0, 128) for j in range(6)]
        for u in range(17):
            pieces = []
            for zp in range(2 if u < 16 else 1):
                for kx in range(3):
                    a = vf[z0 + 2 * u + zp, pl.ds(x0 + kx, 8, 4), :]
                    b = vf[z0 + 2 * u + zp, pl.ds(x0 + kx + 2, 8, 4), :]
                    p = jnp.concatenate([a, b], axis=0)
                    pieces.append(pltpu.roll(p.astype(BF16), shift[zp * 3 + kx], 1))
            for h in range(2):
                v = pieces[-1]
                for j in reversed(range(len(pieces) - 1)):
                    v = jnp.where(masks[h][j], pieces[j], v)
                ub[slot, h, u] = v

    bias = jnp.concatenate([sb[...], sb[...]], axis=1)

    def stem(pf, site, slots):
        for h in range(2):
            lhs = jnp.concatenate(
                [
                    jnp.concatenate([ub[t, h, 0:16].reshape(256, 128), ub[t, h, 1:17].reshape(256, 128)], axis=1)
                    for t in slots
                ],
                axis=0,
            )
            for pair in range(2):
                at = (h * 2 + pair) * 256
                r = jnp.dot(lhs, ws[:, at : at + 256], preferred_element_type=F32)
                r = r.reshape(len(slots), 8, 4, 8, 256)
                m = jnp.maximum(jnp.maximum(r[:, :, 0], r[:, :, 1]), jnp.maximum(r[:, :, 2], r[:, :, 3]))
                m = jnp.maximum(m[..., 0:128], m[..., 128:256])
                v = jnp.maximum(m + bias[None, None], 0.0)
                for t in range(len(slots)):
                    for z in range(8):
                        pf[z, h * 2 + pair, pl.ds(site + t, 8, GROUP + 1), :] = v[t, z]

    low = lanes_of((sites, 128)) < 64

    def halo(v, mask):
        r = [pltpu.roll(t, 64, 1) for t in v]
        zero = jnp.zeros_like(r[0])
        return [jnp.where(mask, r[p - 1] if p > 0 else zero, r[p + 1] if p < 3 else zero) for p in range(4)]

    low16 = lanes_of((GROUP, 128)) < 64

    def pack(pf, z, group):
        at = slice(group * GROUP, (group + 1) * GROUP)
        for x in range(8):
            v = [pf[z, p, x * (GROUP + 1) : x * (GROUP + 1) + GROUP, :].astype(BF16) for p in range(4)]
            q = halo(v, low16)
            for p in range(4):
                pq1[z, x, p, at, 0:128] = v[p]
                pq1[z, x, p, at, 128:256] = q[p]

    for t in range(4):
        build(t, t)
    pfs = (pf0, pf1)
    for group in range(sites // GROUP):
        pf, done = pfs[group % 2], pfs[(group + 1) % 2]

        def eight(i, c, group=group, pf=pf, done=done):
            s = group * GROUP + 8 * i
            for part in range(2):
                for t in range(4):
                    build(jnp.minimum(s + 4 * part + 4 + t, sites - 1), 4 * (1 - part) + t)
                for t in (0, 2):
                    stem(pf, 8 * i + 4 * part + t, (4 * part + t, 4 * part + t + 1))
                if group > 0:
                    for z in range(2):
                        pack(done, 4 * i + 2 * part + z, group - 1)
            return c

        lax.fori_loop(0, GROUP // 8, eight, 0)

    def last(z, c):
        pack(pfs[(sites // GROUP - 1) % 2], z, sites // GROUP - 1)
        return c

    for z in range(8):
        last(z, 0)

    def conv(src, big, z, dzs, xb, nz):
        xis = [xi for xi in range(4) if 0 <= 2 * xb - 1 + xi < 8]
        total = None
        for dz in dzs:
            for xi in xis:
                lhs = src[pl.ds(z + dz - 1, nz), 2 * xb - 1 + xi].reshape(nz * 4 * sites, 256)
                part = jnp.dot(lhs, big[dz * 4 + xi], preferred_element_type=F32)
                total = part if total is None else total + part
        return total

    bias1 = jnp.concatenate([b1[...]] * 4, axis=1)
    bias2 = jnp.concatenate([b2[...]] * 4, axis=1)

    def first(z, dzs, nz):
        for xb in range(4):
            v = jnp.maximum(conv(pq1, big1, z, dzs, xb, nz) + bias1, 0.0).reshape(nz, 4, sites, 256)
            for k in range(nz):
                for xo in range(2):
                    t = [v[k, p, :, xo * 128 : xo * 128 + 128].astype(BF16) for p in range(4)]
                    q = halo(t, low)
                    for p in range(4):
                        pq2[z + k, 2 * xb + xo, p, :, 0:128] = t[p]
                        pq2[z + k, 2 * xb + xo, p, :, 128:256] = q[p]

    def second(z, dzs, nz):
        for xb in range(4):
            v = conv(pq2, big2, z, dzs, xb, nz) + bias2
            skip = jnp.concatenate(
                [pq1[pl.ds(z, nz), 2 * xb + xo, :, :, 0:128].reshape(nz * 4 * sites, 128) for xo in range(2)], axis=1
            )
            v = jnp.maximum(v + skip.astype(F32), 0.0).reshape(nz * 4, sites, 256)
            acc[...] += jnp.sum(v, axis=0)

    def over_z(step):
        step(0, (1, 2), 1)
        step(1, (0, 1, 2), 3)
        step(4, (0, 1, 2), 3)
        step(7, (0, 1), 1)

    over_z(first)
    acc[...] = jnp.zeros_like(acc)
    over_z(second)
    a = acc[...]
    mean = (a[:, 0:64] + a[:, 64:128] + a[:, 128:192] + a[:, 192:256]) * (1.0 / 512.0)
    own = jnp.dot(mean, hw[...].astype(F32), precision=lax.Precision.HIGHEST, preferred_element_type=F32) + hb[...]
    half = sites // 2
    out[0:half, :] = jnp.concatenate([own[0:half], own[half:]], axis=1)
    names = jnp.concatenate([dest[...].astype(F32), ids[...].astype(F32)], axis=1)
    out[half : half + 8, :] = jnp.broadcast_to(names, (8, 128))


def embed(volume, corners, destination, svx_ids, stem_w, stem_b, conv_w1, conv_b1, conv_w2, conv_b2, head_w, head_b):
    sites = corners.shape[1]
    sw = stem_w.transpose(0, 1, 3, 2, 4).reshape(9, 3, 64)
    vmem = pl.BlockSpec(memory_space=pltpu.VMEM)
    hbm = pl.BlockSpec(memory_space=pl.ANY)
    smem = pl.BlockSpec(memory_space=pltpu.SMEM)
    return pl.pallas_call(
        functools.partial(kernel, sites),
        out_shape=jax.ShapeDtypeStruct((sites // 2 + 8, 128), F32),
        in_specs=[smem, hbm, vmem, vmem, hbm, vmem, hbm] + [vmem] * 5,
        out_specs=vmem,
        scratch_shapes=[
            pltpu.VMEM((128, 136, 128), F32),
            pltpu.VMEM((8, 2, 17, 16, 128), BF16),
            pltpu.VMEM((32, 64), F32),
            pltpu.VMEM((8, 4, 8 * (GROUP + 1) + GROUP, 128), F32),
            pltpu.VMEM((8, 4, 8 * (GROUP + 1) + GROUP, 128), F32),
            pltpu.VMEM((8, 8, 4, sites, 256), BF16),
            pltpu.VMEM((8, 8, 4, sites, 256), BF16),
            pltpu.VMEM((256, 1024), BF16),
            pltpu.VMEM((12, 256, 256), BF16),
            pltpu.VMEM((12, 256, 256), BF16),
            pltpu.VMEM((sites, 256), F32),
            pltpu.VMEM((128, 128, 128), BF16),
            pltpu.VMEM((27, 64, 64), BF16),
            pltpu.VMEM((27, 64, 64), BF16),
            pltpu.SemaphoreType.DMA((10,)),
        ],
        compiler_params=pltpu.CompilerParams(vmem_limit_bytes=60 * 1024 * 1024),
        cost_estimate=pl.CostEstimate(flops=30_000_000_000, bytes_accessed=6_000_000, transcendentals=0),
    )(
        corners, volume, sw, stem_b.reshape(1, 64), conv_w1.reshape(27, 64, 64), conv_b1.reshape(1, 64),
        conv_w2.reshape(27, 64, 64), conv_b2.reshape(1, 64), head_w, head_b.reshape(1, 64),
        destination.reshape(1, sites), svx_ids.reshape(1, sites),
    )


def collect_kernel(n_xy, own_rows, source_of, me_ref, table, *refs):
    pieces, (batch, sums, hots) = refs[:-3], refs[-3:]
    me = me_ref[0]
    size = pieces[0].shape[0]
    blocks = [(p, r) for p in pieces for r in range(0, size, 40)]
    names = jnp.concatenate([p[r + 32 : r + 33, :] for p, r in blocks], axis=0).astype(jnp.int32)
    dest, ids = names[:, 0:64], names[:, 64:128]
    valid = (dest == me).astype(F32)
    earlier = (lax.broadcasted_iota(jnp.int32, (64, 64), 0) < lax.broadcasted_iota(jnp.int32, (64, 64), 1)).astype(F32)
    rank = jnp.dot(valid, earlier, preferred_element_type=F32).astype(jnp.int32)
    source = jnp.concatenate([jnp.full((1, 64), k, jnp.int32) for k in source_of], axis=0)
    row = jnp.where(dest == me, jnp.bitwise_xor(source, me) * 4 + rank, -1)
    t = table[...]
    want = lax.broadcasted_iota(jnp.int32, (own_rows, 128), 0) + me * own_rows
    found = jnp.zeros((own_rows, 128), jnp.int32)
    lane = lax.broadcasted_iota(jnp.int32, (own_rows, 128), 1)
    for r in range(t.shape[0]):
        found = found + jnp.where(t[r : r + 1, :] == want, lane + r * 128, 0)
    owned = jnp.sum(found, axis=1, keepdims=True)
    rows = lax.broadcasted_iota(jnp.int32, (own_rows, 128), 0)
    for g in range(n_xy // 4):
        for half in range(2):
            cut = slice(half * 32, half * 32 + 32)
            w, s = [jnp.concatenate([x[q : q + 1, cut] for q in range(4 * g, 4 * g + 4)], axis=1) for x in (row, ids)]
            top = half * 2 * own_rows
            at = slice(g * 128, g * 128 + 128)
            hots[top : top + own_rows, at] = (rows == w).astype(F32).astype(BF16)
            hots[top + own_rows : top + 2 * own_rows, at] = (owned == s).astype(F32).astype(BF16)
    x = jnp.concatenate([p[r : r + 32, :] for p, r in blocks], axis=0)
    hi = x.astype(BF16)
    rest = x - hi.astype(F32)
    mid = rest.astype(BF16)
    low = (rest - mid.astype(F32)).astype(BF16)
    total = jnp.dot(hots[...], jnp.concatenate([hi, mid, low], axis=1), preferred_element_type=F32)
    total = total[:, 0:128] + (total[:, 128:256] + total[:, 256:384])
    n = own_rows
    both = [total[a : a + n, 0:64] + total[a + 2 * n : a + 3 * n, 64:128] for a in (0, n)]
    turned = jnp.concatenate(both, axis=1).T
    batch[...] = turned[0:64]
    sums[...] = turned[64:128]


def collect(pieces, source_of, table, me, n_xy):
    own_rows = table.size // n_xy
    vmem = pl.BlockSpec(memory_space=pltpu.VMEM)
    return pl.pallas_call(
        functools.partial(collect_kernel, n_xy, own_rows, source_of),
        out_shape=(jax.ShapeDtypeStruct((64, own_rows), F32),) * 2,
        in_specs=[pl.BlockSpec(memory_space=pltpu.SMEM)] + [vmem] * (1 + len(pieces)),
        out_specs=(vmem, vmem),
        scratch_shapes=[pltpu.VMEM((4 * own_rows, n_xy * 32), BF16)],
        compiler_params=pltpu.CompilerParams(vmem_limit_bytes=32 * 1024 * 1024),
    )(me, table, *pieces)


def body(
    volume, corners, destination, svx_ids, svx_rows,
    stem_w, stem_b, conv_w1, conv_b1, conv_w2, conv_b2, head_w, head_b,
):
    n_xy, n_gz = lax.axis_size("xy"), lax.axis_size("gz")

    def swap(a, k, axis="xy", n=n_xy):
        return lax.ppermute(a, axis, [(i, i ^ k) for i in range(n)])

    own = embed(
        volume, corners, destination, svx_ids, stem_w, stem_b, conv_w1, conv_b1, conv_w2, conv_b2, head_w, head_b
    )
    a = jnp.concatenate([own] + [swap(own, k) for k in (2, 4, 6)])
    pieces = [a] + [swap(a, k) for k in (8, 16, 24)]
    pieces = pieces + [swap(p, 1) for p in pieces]
    source_of = [c + x + y for c in (0, 1) for x in (0, 8, 16, 24) for y in (0, 2, 4, 6)]
    me = lax.axis_index("xy").astype(jnp.int32).reshape(1)
    batch, part = collect(pieces, source_of, svx_rows.reshape(-1, 128), me, n_xy)
    z = [part] + [swap(part, k, "gz", n_gz) for k in (1, 2, 3)]
    return ((z[0] + z[1]) + (z[2] + z[3])).T, batch.T


def solution(mesh):
    sites = P(("gz", "xy"))
    placed = (P("gz", "xy", None), P(None, ("gz", "xy")), P(("gz", "xy"), None), sites) + (P(),) * 9
    return jax.shard_map(
        body, mesh=mesh, in_specs=placed, out_specs=(P("xy", None), P(("gz", "xy"), None)), check_vma=False
    )
```
